256 devices in a mesh: dp: 128 (over x, y_lo, z, core), tensor: 2 (over y_hi).
Axes of the slice: x: 4, y: 4 (y_hi: 2, y_lo: 2; y = y_hi * 2 + y_lo), z: 8, core: 2. Of those that a mesh axis runs over, the one named last changes fastest.
Arguments:
- hidden: bfloat16 [147456, 320], P('dp', 'tensor'), may hold values from -0.4375 to 0.4375
- cotangent: bfloat16 [147456, 4096], P('dp', 'tensor'), may hold values from -6 to 6
- down_weight: bfloat16 [320, 4096], P('tensor'), may hold values from -0.09375 to 0.09375
- momentum: float32 [128, 320, 4096], P('dp', 'tensor'), may hold values from -6 to 6
Outputs:
- update: bfloat16 [320, 4096], P('tensor')
- momentum_out: float32 [128, 320, 4096], P('dp', 'tensor')
- hidden_grad: bfloat16 [147456, 320], P('dp', 'tensor')
The draws below stay inside these ranges and needn't reach their ends.
All inputs are finite; a program needn't handle non-finite values.
Results may differ from the reference program's by a relative error of at most 0.001.
Values may be sent and summed in bfloat16 or wider, within the bound.
No kernel may reach another device: no remote copies, remote signals or barrier semaphores. Data moves between devices by JAX's collectives and lax.ppermute only.
A program may use at most 128 MiB of HBM per device.

```python
import jax
import jax.numpy as jnp
from jax import lax

D = 4096
BLOCK = 256
BAND = 8
TOK_DEV = 1152
FF_W = 320
TOKENS = 147456
N_DP = 128


def level_of(own_key, dims, split, low, top_value):
    level = 1.0
    for axis_at, parts in split:
        heights = jax.random.uniform(jax.random.fold_in(jax.random.fold_in(own_key, 6), axis_at), (parts,), jnp.float32, low / len(split), top_value / len(split))
        level = level * jnp.repeat(jnp.exp(heights), dims[axis_at] // parts).reshape((-1,) + (1,) * (len(dims) - 1 - axis_at))
    return level


def gaussian(stream_key, dims, deviation, limit, split=(), kind=jnp.bfloat16):
    gain = level_of(stream_key, dims, split, -0.22, 0.18) if split else 1.0
    entries = jax.random.normal(stream_key, dims, jnp.float32) * deviation * gain
    return jnp.minimum(jnp.maximum(entries, -limit), limit).astype(kind)


def setup_inputs(seed: int = 0) -> dict:
    arg_keys = jax.random.split(jax.random.key(seed), 5)
    hidden = gaussian(arg_keys[0], (TOKENS, FF_W), (TOK_DEV ** -0.5), 0.4375, ((0, 128), (1, 2)))
    cotangent = gaussian(arg_keys[1], (TOKENS, D), 1.0, 6.0, ((0, 128), (1, 2)))
    down_weight = gaussian(arg_keys[2], (FF_W, D), D ** -0.5, 0.09375, ((0, 2),))
    momentum = gaussian(arg_keys[3], (N_DP, FF_W, D), 1.0, 6.0, ((0, 128), (1, 2)), jnp.float32)
    return dict(hidden=hidden, cotangent=cotangent, down_weight=down_weight, momentum=momentum)


decay_rate = 0.9

def cosine_table():
    freq = jnp.arange(BAND, dtype=jnp.float32)[:, None]
    place = jnp.arange(BLOCK, dtype=jnp.float32)[None, :]
    scales = jnp.where(freq == 0.0, jnp.sqrt(1.0 / BLOCK), jnp.sqrt(2.0 / BLOCK))
    return (scales * jnp.cos(jnp.pi * (place + 0.5) * freq / BLOCK)).astype(jnp.float32)

def encode(accumulated, cosines):
    flattened = accumulated.reshape(-1, BLOCK)
    return lax.dot_general(cosines, flattened, (((1,), (1,)), ((), ())), precision=lax.Precision.HIGHEST)

def decode(coefficients, cosines, row_count):
    blocks = lax.dot_general(coefficients, cosines, (((0,), (0,)), ((), ())), precision=lax.Precision.HIGHEST)
    return blocks.reshape(row_count, D)

def reference(hidden, cotangent, down_weight, momentum):
    cosines = cosine_table()
    hidden_grad = lax.dot_general(cotangent, down_weight, (((1,), (1,)), ((), ())), preferred_element_type=jnp.float32).astype(jnp.bfloat16)
    hidden_split = hidden.reshape(N_DP, TOK_DEV, FF_W)
    cotangent_split = cotangent.reshape(N_DP, TOK_DEV, D)

    def worker_step(operands):
        hidden_rows, cotangent_rows, momentum_rows = operands
        gradient = lax.dot_general(hidden_rows, cotangent_rows, (((0,), (0,)), ((), ())), preferred_element_type=jnp.float32)
        accumulated = decay_rate * momentum_rows + gradient
        coefficients = encode(accumulated, cosines)
        remainder = accumulated - decode(coefficients, cosines, FF_W)
        return (remainder, coefficients)
    remainder, coefficients = lax.map(worker_step, (hidden_split, cotangent_split, momentum))
    summed = lax.optimization_barrier(jnp.sum(coefficients, axis=0))
    update = decode(summed, cosines, FF_W).astype(jnp.bfloat16)
    return (update, remainder, hidden_grad)
```

```python
import jax
import jax.numpy as jnp
import numpy as np
from jax import lax
from jax.experimental import pallas as pl
from jax.experimental.pallas import tpu as pltpu
from jax.sharding import Mesh
from jax.sharding import PartitionSpec as P

BLOCK = 256
BAND = 8
FINE = ("x", "ylo", "z", "core", "tensor")
FINE_SIZES = (4, 2, 8, 2, 2)
DP = ("x", "ylo", "z", "core")
PLANE = ("x", "ylo")
LINE = ("z", "core", "tensor")
GRANT = 48 * 1024 * 1024

decay_rate = 0.9


def cosine_table():
    freq = np.arange(BAND, dtype=np.float64)[:, None]
    place = np.arange(BLOCK, dtype=np.float64)[None, :]
    scales = np.where(freq == 0.0, np.sqrt(1.0 / BLOCK), np.sqrt(2.0 / BLOCK))
    return scales * np.cos(np.pi * (place + 0.5) * freq / BLOCK)


def halves(table):
    high = table.astype(np.float32).astype(jnp.bfloat16)
    low = (table - high.astype(np.float64)).astype(np.float32).astype(jnp.bfloat16)
    return high, low


def split(value):
    high = value.astype(jnp.bfloat16)
    low = (value - high.astype(jnp.float32)).astype(jnp.bfloat16)
    return high, low


def dot(left, right):
    return jnp.dot(left, right, preferred_element_type=jnp.float32)


def dot_t(left, right):
    return lax.dot_general(left, right, (((1,), (1,)), ((), ())), preferred_element_type=jnp.float32)


def encode(high, low, cosines):
    both = dot_t(cosines, high) + dot_t(cosines, low)
    return both[:BAND] + both[BAND:]


def band_of(high, low, projection_ref):
    return (
        dot(high, projection_ref[0]) + dot(low, projection_ref[0]) + dot(high, projection_ref[1])
    )


def own_kernel(
    place_ref, hidden_ref, cotangent_ref, weight_ref, near_ref, far_ref, cosines_ref,
    projection_ref, remainder_ref, partial_ref, coefficients_ref,
):
    t = place_ref[0]
    tile = cotangent_ref[...]
    accumulated = decay_rate * near_ref[...] + dot(hidden_ref[...], tile)
    high, low = split(accumulated)
    remainder_ref[...] = accumulated - band_of(high, low, projection_ref)
    coefficients_ref[0, t] = encode(high, low, cosines_ref[...])
    high, low = split(decay_rate * far_ref[...])
    coefficients_ref[0, 1 - t] = encode(high, low, cosines_ref[...])
    partial = dot_t(weight_ref[...], tile)

    @pl.when(pl.program_id(0) == 0)
    def _():
        partial_ref[...] = partial

    @pl.when(pl.program_id(0) > 0)
    def _():
        partial_ref[...] += partial


def gradient_kernel(hidden_ref, cotangent_ref, coefficients_ref, cosines_ref, gradient_ref, band_ref):
    gradient = dot(hidden_ref[...], cotangent_ref[...])
    gradient_ref[...] = gradient
    band_ref[0, :2] = coefficients_ref[0]
    band_ref[0, 2] = encode(*split(gradient), cosines_ref[...])


def partial_kernel(place_ref, first_ref, second_ref, cotangent_ref, partial_ref):
    step = pl.program_id(0)
    half = pl.num_programs(0) // 2
    weight = jnp.where(step < half, first_ref[...], second_ref[...])
    partial = dot_t(weight, cotangent_ref[...])

    @pl.when(step == 0)
    def _():
        partial_ref[...] = partial

    @pl.when(step > 0)
    def _():
        partial_ref[...] += partial


def far_kernel(place_ref, held_ref, far_ref, gradient_ref, projection_ref, remainder_ref):
    accumulated = decay_rate * far_ref[...] + gradient_ref[...]
    high, low = split(accumulated)
    remainder_ref[...] = accumulated - band_of(high, low, projection_ref)


def update_kernel(summed_ref, cosines_ref, update_ref):
    for block in range(summed_ref.shape[0] * 2):
        update_ref[:, block * BLOCK : (block + 1) * BLOCK] = lax.dot_general(
            summed_ref[block % 8, block // 8], cosines_ref[...], (((0,), (0,)), ((), ())),
            precision=lax.Precision.HIGHEST, preferred_element_type=jnp.float32,
        ).astype(jnp.bfloat16)


def body(hidden, cotangent, down_weight, momentum):
    f32 = jnp.float32
    rows, width = down_weight.shape
    tokens, features = cotangent.shape
    tiles = features // BLOCK
    t = lax.axis_index("tensor")
    core = lax.axis_index("core")
    place = jnp.stack([t, core]).astype(jnp.int32)
    momentum = momentum.reshape(rows, width)
    table = cosine_table()
    cosines = jnp.asarray(np.concatenate(halves(table)))
    projection = jnp.asarray(np.stack(halves(table.T @ table)))
    swap = [(0, 1), (1, 0)]
    params = pltpu.CompilerParams(dimension_semantics=("arbitrary",), vmem_limit_bytes=GRANT)

    def grid(scalars, in_specs, out_specs):
        return pltpu.PrefetchScalarGridSpec(
            num_scalar_prefetch=scalars, grid=(tiles,), in_specs=in_specs, out_specs=out_specs
        )

    def whole(shape):
        return pl.BlockSpec(shape, lambda j, *_: (0,) * len(shape))

    near = pl.BlockSpec((rows, BLOCK), lambda j, place: (0, place[0] * tiles + j))
    far = pl.BlockSpec((rows, BLOCK), lambda j, place: (0, (1 - place[0]) * tiles + j))
    tile = pl.BlockSpec((tokens, BLOCK), lambda j, *_: (0, j))
    row_tile = pl.BlockSpec((rows, BLOCK), lambda j, *_: (0, j))

    own_hidden = hidden.T
    their_hidden = lax.ppermute(own_hidden, "tensor", swap)
    half = features // 2
    sent = lax.dynamic_slice(down_weight, (0, (1 - t) * features + core * half), (rows, half))
    first = lax.ppermute(sent, ("ylo", "tensor"), [(0, 3), (3, 0), (1, 2), (2, 1)])
    second = lax.ppermute(first, "core", swap)

    remainder, own_partial, coefficients = pl.pallas_call(
        own_kernel,
        grid_spec=grid(
            1,
            [whole((rows, tokens)), tile, near, near, far, whole((2 * BAND, BLOCK)), whole((2, BLOCK, BLOCK))],
            [near, whole((rows, tokens)), pl.BlockSpec((1, 2, BAND, rows), lambda j, *_: (j, 0, 0, 0))],
        ),
        out_shape=[
            jax.ShapeDtypeStruct((rows, width), f32),
            jax.ShapeDtypeStruct((rows, tokens), f32),
            jax.ShapeDtypeStruct((tiles, 2, BAND, rows), f32),
        ],
        compiler_params=params,
        cost_estimate=pl.CostEstimate(flops=4 * rows * tokens * features, bytes_accessed=12 << 20, transcendentals=0),
        name="own_half",
    )(place, own_hidden, cotangent, down_weight, momentum, momentum, cosines, projection)

    gradient, band = pl.pallas_call(
        gradient_kernel,
        grid_spec=grid(
            0,
            [whole((rows, tokens)), tile, pl.BlockSpec((1, 2, BAND, rows), lambda j: (j, 0, 0, 0)), whole((2 * BAND, BLOCK))],
            [row_tile, pl.BlockSpec((1, 3, BAND, rows), lambda j: (j, 0, 0, 0))],
        ),
        out_shape=[
            jax.ShapeDtypeStruct((rows, features), f32),
            jax.ShapeDtypeStruct((tiles, 3, BAND, rows), f32),
        ],
        compiler_params=params,
        cost_estimate=pl.CostEstimate(flops=2 * rows * tokens * features, bytes_accessed=7 << 20, transcendentals=0),
        name="their_gradient",
    )(their_hidden, cotangent, coefficients, cosines)
    far_gradient = lax.ppermute(gradient, "tensor", swap)

    partial = pl.pallas_call(
        partial_kernel,
        grid_spec=grid(
            1,
            [
                pl.BlockSpec((rows, BLOCK), lambda j, place: (0, jnp.minimum(j, tiles // 2 - 1))),
                pl.BlockSpec((rows, BLOCK), lambda j, place: (0, jnp.maximum(j - tiles // 2, 0))),
                pl.BlockSpec((tokens, BLOCK), lambda j, place: (0, (place[1] * (tiles // 2) + j) % tiles)),
            ],
            whole((rows, tokens)),
        ),
        out_shape=jax.ShapeDtypeStruct((rows, tokens), f32),
        compiler_params=params,
        cost_estimate=pl.CostEstimate(flops=2 * rows * tokens * features, bytes_accessed=6 << 20, transcendentals=0),
        name="their_partial",
    )(place, first, second, cotangent)
    far_partial = lax.ppermute(partial, "tensor", swap)

    spread = lax.all_to_all(band, PLANE, 0, 0, tiled=True)
    total = jnp.sum(spread, axis=0)
    slot = jnp.arange(2)[:, None, None]
    across = jnp.where(slot == t, total[2][None], 0.0)
    partner = (jnp.arange(32) % 2)[:, None, None, None] == t
    payload = jnp.where(partner, total[None, :2], across[None])
    total = jnp.sum(lax.all_to_all(payload, LINE, 0, 0, tiled=True), axis=0)
    payload = jnp.broadcast_to(total[None], (8,) + total.shape)
    summed = lax.all_to_all(payload, PLANE, 0, 0, tiled=True)

    update = pl.pallas_call(
        update_kernel,
        out_shape=jax.ShapeDtypeStruct((rows, width), jnp.bfloat16),
        compiler_params=pltpu.CompilerParams(vmem_limit_bytes=GRANT),
        name="update",
    )(summed, jnp.asarray(table.astype(np.float32)))

    remainder = pl.pallas_call(
        far_kernel,
        grid_spec=grid(
            1,
            [pl.BlockSpec(memory_space=pl.ANY), far, row_tile, whole((2, BLOCK, BLOCK))],
            far,
        ),
        out_shape=jax.ShapeDtypeStruct((rows, width), f32),
        input_output_aliases={1: 0},
        compiler_params=params,
        cost_estimate=pl.CostEstimate(flops=0, bytes_accessed=4 << 20, transcendentals=0),
        name="far_half",
    )(place, remainder, momentum, far_gradient, projection)

    hidden_grad = (own_partial + far_partial).astype(jnp.bfloat16).T
    return (update, remainder[None], hidden_grad)


def solution(mesh):
    fine = Mesh(mesh.devices.reshape(FINE_SIZES), FINE)
    return jax.shard_map(
        body,
        mesh=fine,
        in_specs=(P(DP, "tensor"), P(DP, "tensor"), P("tensor", None), P(DP, "tensor", None)),
        out_specs=(P("tensor", None), P(DP, "tensor", None), P(DP, "tensor")),
        check_vma=False,
    )
```

```python
import jax
import jax.numpy as jnp
import numpy as np
from jax import lax
from jax.experimental import pallas as pl
from jax.experimental.pallas import tpu as pltpu
from jax.sharding import Mesh
from jax.sharding import PartitionSpec as P

BLOCK = 256
BAND = 8
FINE = ("x", "ylo", "z", "core", "tensor")
FINE_SIZES = (4, 2, 8, 2, 2)
DP = ("x", "ylo", "z", "core")
SPACE = ("x", "z", "core")
WIDE = 1024

decay_rate = 0.9


def cosine_table():
    freq = np.arange(BAND, dtype=np.float64)[:, None]
    place = np.arange(BLOCK, dtype=np.float64)[None, :]
    scales = np.where(freq == 0.0, np.sqrt(1.0 / BLOCK), np.sqrt(2.0 / BLOCK))
    return scales * np.cos(np.pi * (place + 0.5) * freq / BLOCK)


def halves(table):
    high = table.astype(np.float32).astype(jnp.bfloat16)
    low = (table - high.astype(np.float64)).astype(np.float32).astype(jnp.bfloat16)
    return high, low


def split(value):
    high = value.astype(jnp.bfloat16)
    low = (value - high.astype(jnp.float32)).astype(jnp.bfloat16)
    return high, low


def dot(left, right):
    return jnp.dot(left, right, preferred_element_type=jnp.float32)


def dot_t(left, right):
    return lax.dot_general(left, right, (((1,), (1,)), ((), ())), preferred_element_type=jnp.float32)


def encode(high, low, cosines):
    both = dot_t(cosines, high) + dot_t(cosines, low)
    return both[:BAND] + both[BAND:]


def band_of(high, low, projection):
    return dot(high, projection[0]) + dot(low, projection[0]) + dot(high, projection[1])


def own_kernel(
    place_ref, hidden_ref, cotangent_ref, weight_ref, momentum_ref, cosines_ref, diagonal_ref, projection_ref,
    remainder_ref, partial_ref, coefficients_ref, encoded_ref, largest_ref,
    held_ref, weight, near, far, left, ready, written,
):
    rows, features = near.shape
    steps, count = features // WIDE, WIDE // BLOCK
    total = features // BLOCK
    t = place_ref[0]
    base = pl.multiple_of(t * features, features)
    other = pl.multiple_of((1 - t) * features, features)
    loads = []
    for step in range(steps):
        at = pl.ds(step * WIDE, WIDE)
        here = pl.ds(pl.multiple_of(base + step * WIDE, WIDE), WIDE)
        there = pl.ds(pl.multiple_of(other + step * WIDE, WIDE), WIDE)
        loads.append([
            pltpu.make_async_copy(source, target, ready.at[step, index])
            for index, (source, target) in enumerate((
                (cotangent_ref.at[:, at], held_ref.at[:, at]),
                (weight_ref.at[:, here], weight.at[:, at]),
                (momentum_ref.at[:, here], near.at[:, at]),
                (momentum_ref.at[:, there], far.at[:, at]),
            ))
        ])
    for step in range(steps):
        for load in loads[step]:
            load.start()
    cosines = cosines_ref[...].astype(jnp.bfloat16)
    projection = projection_ref[...].astype(jnp.bfloat16)
    diagonal = diagonal_ref[...].astype(jnp.bfloat16)
    stores = []
    for step in range(steps):
        at = slice(step * WIDE, (step + 1) * WIDE)
        loads[step][0].wait()
        loads[step][1].wait()
        tile = held_ref[:, at]
        product = dot_t(jnp.concatenate([weight[:, at], diagonal]), tile)
        if step == 0:
            partial_ref[...] = product[:rows]
        else:
            partial_ref[...] += product[:rows]
        for block in range(count):
            first = rows + block * 2 * BAND
            place = (step * count + block) * BAND
            encoded_ref[place : place + BAND] = (
                product[first : first + BAND] + product[first + BAND : first + 2 * BAND]
            )
        largest_ref[:, at] = jnp.max(jnp.abs(tile), axis=0, keepdims=True).astype(jnp.float32)
        gradient = dot(hidden_ref[...], tile)
        loads[step][2].wait()
        loads[step][3].wait()
        for block in range(count):
            own = slice(block * BLOCK, (block + 1) * BLOCK)
            place = slice(step * WIDE + block * BLOCK, step * WIDE + (block + 1) * BLOCK)
            accumulated = decay_rate * near[:, place] + gradient[:, own]
            high, low = split(accumulated)
            left[:, place] = accumulated - band_of(high, low, projection)
            coefficients_ref[t * total + step * count + block] = encode(high, low, cosines)
            high, low = split(decay_rate * far[:, place])
            coefficients_ref[(1 - t) * total + step * count + block] = encode(high, low, cosines)
        here = pl.ds(pl.multiple_of(base + step * WIDE, WIDE), WIDE)
        stores.append(pltpu.make_async_copy(left.at[:, at], remainder_ref.at[:, here], written.at[step]))
        stores[-1].start()
    for store in stores:
        store.wait()


def their_band_kernel(hidden_ref, encoded_ref, largest_ref, band_ref, scale_ref):
    hidden = hidden_ref[...]
    count = encoded_ref.shape[0]
    both = dot_t(jnp.concatenate(split(encoded_ref[...])), hidden)
    band = both[:count] + both[count:]
    for block in range(count // BAND):
        band_ref[block] = band[block * BAND : (block + 1) * BAND]
    bound = jnp.max(largest_ref[...]) * jnp.max(jnp.abs(hidden).astype(jnp.float32))
    bound = bound * hidden.shape[1]
    scale, inverse = 1.0, 1.0
    for power in (64, 32, 16, 8, 4, 2):
        fits = bound * (scale * 2.0**power) <= 32768.0
        scale = jnp.where(fits, scale * 2.0**power, scale)
        inverse = jnp.where(fits, inverse * 2.0**-power, inverse)
    scale_ref[...] = jnp.full(scale_ref.shape, scale, jnp.float32)
    band_ref[count // BAND] = jnp.full(band_ref.shape[1:], inverse, jnp.float32)


def gradient_kernel(hidden_ref, cotangent_ref, scale_ref, gradient_ref, held, ready):
    steps, _, chunk = held.shape
    spots = [slice(step * chunk, (step + 1) * chunk) for step in range(steps)]
    loads = [
        pltpu.make_async_copy(cotangent_ref.at[:, spots[step]], held.at[step], ready.at[step])
        for step in range(steps)
    ]
    for load in loads:
        load.start()
    for step in range(steps):
        loads[step].wait()
        gradient_ref[:, spots[step]] = dot(hidden_ref[...], held[step]) * scale_ref[0:1, 0:1]


def partial_kernel(place_ref, cotangent_ref, first_ref, second_ref, partial_ref, held, ready):
    steps, _, chunk = held.shape
    half = steps // 2
    core = place_ref[1]
    loads = []
    for step in range(steps):
        side = core if step < half else 1 - core
        spot = pl.ds(pl.multiple_of((side * half + step % half) * chunk, chunk), chunk)
        loads.append(pltpu.make_async_copy(cotangent_ref.at[:, spot], held.at[step], ready.at[step]))
        loads[step].start()
    for step in range(steps):
        source = first_ref if step < half else second_ref
        start = step % half * chunk
        loads[step].wait()
        partial = dot_t(source[:, start : start + chunk], held[step])
        if step == 0:
            partial_ref[...] = partial
        else:
            partial_ref[...] += partial


def add_kernel(left_ref, right_ref, total_ref):
    total_ref[...] = (left_ref[...] + right_ref[...]).astype(total_ref.dtype)


def far_kernel(place_ref, held_ref, far_ref, gradient_ref, inverse_ref, projection_ref, remainder_ref):
    accumulated = decay_rate * far_ref[...] + gradient_ref[...] * inverse_ref[0, 0:1, 0:1]
    high, low = split(accumulated)
    projection = projection_ref[...].astype(jnp.bfloat16)
    for block in range(far_ref.shape[1] // BLOCK):
        at = slice(block * BLOCK, (block + 1) * BLOCK)
        remainder_ref[:, at] = accumulated[:, at] - band_of(high[:, at], low[:, at], projection)


def thirds(value):
    first = value.astype(jnp.bfloat16).astype(jnp.float32)
    second = (value - first).astype(jnp.bfloat16).astype(jnp.float32)
    return first, second, value - first - second


def update_kernel(summed_ref, cosines_ref, update_ref):
    cosines = cosines_ref[...].astype(jnp.bfloat16)
    for block in range(summed_ref.shape[0]):
        a, b, c = thirds(summed_ref[block])
        stacked = jnp.concatenate([a, a, b, b, a, c]).T.astype(jnp.bfloat16)
        update_ref[:, block * BLOCK : (block + 1) * BLOCK] = dot(stacked, cosines).astype(jnp.bfloat16)


def call(kernel, name, steps, scalars, in_specs, out_specs, out_shape, flops, size, grant=20, **more):
    return pl.pallas_call(
        kernel,
        grid_spec=pltpu.PrefetchScalarGridSpec(
            num_scalar_prefetch=scalars, grid=(steps,), in_specs=in_specs, out_specs=out_specs
        ),
        out_shape=out_shape,
        compiler_params=pltpu.CompilerParams(
            dimension_semantics=("arbitrary",), vmem_limit_bytes=grant << 20
        ),
        cost_estimate=pl.CostEstimate(flops=flops, bytes_accessed=size, transcendentals=0),
        name=name,
        **more,
    )


def whole(shape):
    return pl.BlockSpec(shape, lambda *_: (0,) * len(shape))


def shape_of(*shape, dtype=jnp.float32):
    return jax.ShapeDtypeStruct(shape, dtype)


def tables():
    table = cosine_table()
    high, low = halves(table)
    rest = table - high.astype(np.float64) - low.astype(np.float64)
    third = rest.astype(np.float32).astype(jnp.bfloat16)
    cosines = np.concatenate([high, low])
    diagonal = np.zeros((WIDE // BLOCK, 2 * BAND, WIDE // BLOCK, BLOCK), cosines.dtype)
    for block in range(WIDE // BLOCK):
        diagonal[block, :, block] = cosines
    arrays = (
        cosines,
        diagonal.reshape(-1, WIDE),
        np.stack(halves(table.T @ table)),
        np.concatenate([high, low, high, low, third, high]),
    )
    return [array.astype(np.float32) for array in arrays]


def body(hidden, cotangent, down_weight, momentum):
    rows, width = down_weight.shape
    tokens, features = cotangent.shape
    blocks, steps = features // BLOCK, features // WIDE
    flops = 2 * rows * tokens * features
    t = lax.axis_index("tensor")
    core = lax.axis_index("core")
    place = jnp.stack([t, core]).astype(jnp.int32)
    momentum = momentum.reshape(rows, width)
    cosines, diagonal, projection, decoder = tables()
    swap = [(0, 1), (1, 0)]
    cross = [(0, 3), (3, 0), (1, 2), (2, 1)]

    near = pl.BlockSpec((rows, WIDE), lambda j, place: (0, place[0] * steps + j))
    far = pl.BlockSpec((rows, WIDE), lambda j, place: (0, (1 - place[0]) * steps + j))
    tile = pl.BlockSpec((tokens, WIDE), lambda j, *_: (0, j))
    row_tile = pl.BlockSpec((rows, WIDE), lambda j, *_: (0, j))

    own_hidden = hidden.T
    their_hidden = lax.ppermute(own_hidden, "tensor", swap)
    half = features // 2
    sent = lax.dynamic_slice(down_weight, (0, (1 - t) * features + core * half), (rows, half))
    first = lax.ppermute(sent, ("ylo", "tensor"), cross)
    smem = pl.BlockSpec(memory_space=pltpu.SMEM)
    vmem = pl.BlockSpec(memory_space=pltpu.VMEM)
    hbm = pl.BlockSpec(memory_space=pl.ANY)
    remainder, own_partial, own_band, encoded, largest = pl.pallas_call(
        own_kernel,
        in_specs=[smem, vmem, hbm, hbm, hbm, vmem, vmem, vmem],
        out_specs=[hbm] + [vmem] * 4,
        out_shape=[
            shape_of(rows, width), shape_of(rows, tokens), shape_of(2 * blocks, BAND, rows),
            shape_of(blocks * BAND, tokens), shape_of(1, features),
        ],
        scratch_shapes=[
            pltpu.VMEM((tokens, features), cotangent.dtype),
            pltpu.VMEM((rows, features), down_weight.dtype), pltpu.VMEM((rows, features), jnp.float32),
            pltpu.VMEM((rows, features), jnp.float32), pltpu.VMEM((rows, features), jnp.float32),
            pltpu.SemaphoreType.DMA((steps, 4)), pltpu.SemaphoreType.DMA((steps,)),
        ],
        compiler_params=pltpu.CompilerParams(vmem_limit_bytes=53 << 20),
        cost_estimate=pl.CostEstimate(flops=2 * flops, bytes_accessed=12 << 20, transcendentals=0),
        name="own_half",
    )(place, own_hidden, cotangent, down_weight, momentum, cosines, diagonal, projection)
    near_band = lax.ppermute(own_band, "ylo", swap)

    their_band, scale = call(
        their_band_kernel, "their_band", 1, 0,
        [whole((rows, tokens)), whole((blocks * BAND, tokens)), whole((1, features))],
        [whole((blocks + 1, BAND, rows)), whole((8, 128))],
        [shape_of(blocks + 1, BAND, rows), shape_of(8, 128)],
        4 * rows * tokens * blocks * BAND, 1 << 20, grant=8,
    )(their_hidden, encoded, largest)
    far_band = lax.ppermute(their_band, "tensor", swap)
    cross_band = lax.ppermute(their_band, ("ylo", "tensor"), cross)

    first, scale = lax.optimization_barrier((first, scale))
    second = lax.ppermute(first, "core", swap)
    scratch = [pltpu.VMEM((4, tokens, features // 4), cotangent.dtype), pltpu.SemaphoreType.DMA((4,))]
    gradient = pl.pallas_call(
        gradient_kernel,
        in_specs=[vmem, hbm, vmem],
        out_specs=vmem,
        out_shape=shape_of(rows, features),
        scratch_shapes=scratch,
        compiler_params=pltpu.CompilerParams(vmem_limit_bytes=53 << 20),
        cost_estimate=pl.CostEstimate(flops=flops, bytes_accessed=6 << 20, transcendentals=0),
        name="their_gradient",
    )(their_hidden, cotangent, scale)
    gradient, near_band, far_band, cross_band = lax.optimization_barrier(
        (gradient, near_band, far_band, cross_band)
    )
    gradient = gradient.astype(jnp.float16)
    far_gradient = lax.ppermute(gradient, "tensor", swap)

    slot = jnp.arange(2)[:, None, None, None]
    received = (far_band + cross_band)[None, :blocks]
    total = (own_band + near_band).reshape(2, blocks, BAND, rows)
    total = total + jnp.where(slot == t, 0.0, received)
    total = total.reshape(64, -1, rows)
    total, gradient = lax.optimization_barrier((total, gradient))
    total = lax.all_to_all(total, SPACE, 0, 0, tiled=True)

    second, far_gradient = lax.optimization_barrier((second, far_gradient))
    partial = pl.pallas_call(
        partial_kernel,
        in_specs=[smem, hbm, vmem, vmem],
        out_specs=vmem,
        out_shape=shape_of(rows, tokens),
        scratch_shapes=scratch,
        compiler_params=pltpu.CompilerParams(vmem_limit_bytes=53 << 20),
        cost_estimate=pl.CostEstimate(flops=1 << 20, bytes_accessed=1 << 12, transcendentals=0),
        name="their_partial",
    )(place, cotangent, first, second)
    total, partial = lax.optimization_barrier((total, partial))
    far_partial = lax.ppermute(partial, "tensor", swap)
    total = jnp.sum(total, axis=0)
    far_gradient = far_gradient.astype(jnp.float32)
    total = lax.all_to_all(jnp.broadcast_to(total[None], (64,) + total.shape), SPACE, 0, 0, tiled=True)
    summed = total.reshape(2 * blocks, BAND, rows)

    remainder = call(
        far_kernel, "far_half", steps, 1,
        [
            pl.BlockSpec(memory_space=pl.ANY), far, row_tile,
            pl.BlockSpec((1, BAND, rows), lambda j, place: (blocks, 0, 0)), whole(projection.shape),
        ],
        far, shape_of(rows, width), 1 << 20, 1 << 12, input_output_aliases={1: 0},
    )(place, remainder, momentum, far_gradient, far_band, projection)

    summed, remainder = lax.optimization_barrier((summed, remainder))
    update = call(
        update_kernel, "update", 1, 0, [whole(summed.shape), whole(decoder.shape)],
        whole((rows, width)), shape_of(rows, width, dtype=jnp.bfloat16), 1 << 29, 2 << 20, grant=8,
    )(summed, decoder)

    hidden_grad = call(
        add_kernel, "add", 1, 0, [whole((rows, tokens))] * 2, whole((rows, tokens)),
        shape_of(rows, tokens, dtype=jnp.bfloat16), 1 << 18, 2 << 20,
    )(own_partial, far_partial).T
    return (update, remainder[None], hidden_grad)


def solution(mesh):
    fine = Mesh(mesh.devices.reshape(FINE_SIZES), FINE)
    return jax.shard_map(
        body,
        mesh=fine,
        in_specs=(P(DP, "tensor"), P(DP, "tensor"), P("tensor", None), P(DP, "tensor", None)),
        out_specs=(P("tensor", None), P(DP, "tensor", None), P(DP, "tensor")),
        check_vma=False,
    )
```

```python
import jax
import jax.numpy as jnp
import numpy as np
from jax import lax
from jax.experimental import pallas as pl
from jax.experimental.pallas import tpu as pltpu
from jax.sharding import Mesh
from jax.sharding import PartitionSpec as P

BLOCK = 256
BAND = 8
FINE = ("x", "ylo", "z", "core", "tensor")
FINE_SIZES = (4, 2, 8, 2, 2)
DP = ("x", "ylo", "z", "core")
SPACE = ("x", "z", "core")

decay_rate = 0.9


def cosine_table():
    freq = np.arange(BAND, dtype=np.float64)[:, None]
    place = np.arange(BLOCK, dtype=np.float64)[None, :]
    scales = np.where(freq == 0.0, np.sqrt(1.0 / BLOCK), np.sqrt(2.0 / BLOCK))
    return scales * np.cos(np.pi * (place + 0.5) * freq / BLOCK)


def halves(table):
    high = table.astype(np.float32).astype(jnp.bfloat16)
    low = (table - high.astype(np.float64)).astype(np.float32).astype(jnp.bfloat16)
    return high, low


def split(value):
    high = value.astype(jnp.bfloat16)
    low = (value - high.astype(jnp.float32)).astype(jnp.bfloat16)
    return high, low


def dot(left, right):
    return jnp.dot(left, right, preferred_element_type=jnp.float32)


def dot_t(left, right):
    return lax.dot_general(left, right, (((1,), (1,)), ((), ())), preferred_element_type=jnp.float32)


def encode(high, low, cosines):
    both = dot_t(cosines, high) + dot_t(cosines, low)
    return both[:BAND] + both[BAND:]


def band_of(high, low, projection):
    return dot(high, projection[0]) + dot(low, projection[0]) + dot(high, projection[1])


def own_band_kernel(
    place_ref, hidden_ref, cotangent_ref, momentum_ref, cosines_ref,
    coefficients_ref, encoded_ref, largest_ref, held_ref, carried, hidden, table, ready, landed, arrived,
):
    steps, features = carried.shape[0], cotangent_ref.shape[1]
    chunk = features // steps
    count, total = chunk // BLOCK, features // BLOCK
    t = place_ref[0]
    loads, moves = [], []
    for step in range(steps):
        at = pl.ds(step * chunk, chunk)
        loads.append(pltpu.make_async_copy(cotangent_ref.at[:, at], held_ref.at[:, at], ready.at[step]))
    for step in range(steps):
        at = pl.ds(step * carried.shape[2], carried.shape[2])
        moves.append(pltpu.make_async_copy(momentum_ref.at[:, at], carried.at[step], landed.at[step]))
    extra = [
        pltpu.make_async_copy(cosines_ref, table, arrived.at[0]),
        pltpu.make_async_copy(hidden_ref, hidden, arrived.at[1]),
    ]
    for copy in extra[:1] + loads + moves + extra[1:]:
        copy.start()
    extra[0].wait()
    cosines = table[...].astype(jnp.bfloat16)
    for step in range(steps):
        loads[step].wait()
        at = slice(step * chunk, (step + 1) * chunk)
        largest_ref[:, at] = jnp.max(jnp.abs(held_ref[:, at]), axis=0, keepdims=True).astype(jnp.float32)
        for block in range(count):
            place = step * count + block
            both = dot_t(cosines, held_ref[:, place * BLOCK : (place + 1) * BLOCK])
            at = place * BAND
            encoded_ref[at : at + BAND] = both[:BAND] + both[BAND:]
    for step in range(steps):
        moves[step].wait()
        for block in range(carried.shape[2] // BLOCK):
            high, low = split(decay_rate * carried[step, :, block * BLOCK : (block + 1) * BLOCK])
            coefficients_ref[step * (carried.shape[2] // BLOCK) + block] = encode(high, low, cosines)
    extra[1].wait()
    both = dot_t(jnp.concatenate(split(encoded_ref[...])), hidden[...])
    band = both[: total * BAND] + both[total * BAND :]
    for block in range(total):
        coefficients_ref[t * total + block] += band[block * BAND : (block + 1) * BAND]


def their_band_kernel(hidden_ref, encoded_ref, largest_ref, band_ref, scale_ref):
    hidden = hidden_ref[...]
    count = encoded_ref.shape[0]
    both = dot_t(jnp.concatenate(split(encoded_ref[...])), hidden)
    band = both[:count] + both[count:]
    for block in range(count // BAND):
        band_ref[block] = band[block * BAND : (block + 1) * BAND]
    bound = jnp.max(largest_ref[...]) * jnp.max(jnp.abs(hidden).astype(jnp.float32))
    bound = bound * hidden.shape[1]
    scale, inverse = 1.0, 1.0
    for power in (64, 32, 16, 8, 4, 2):
        fits = bound * (scale * 2.0**power) <= 32768.0
        scale = jnp.where(fits, scale * 2.0**power, scale)
        inverse = jnp.where(fits, inverse * 2.0**-power, inverse)
    scale_ref[...] = jnp.full(scale_ref.shape, scale, jnp.float32)
    band_ref[count // BAND] = jnp.full(band_ref.shape[1:], inverse, jnp.float32)


def gradients_kernel(
    their_ref, own_ref, held_ref, scale_ref, gradient_ref, own_gradient_ref, own, gradient, arrived, written
):
    rows, features = gradient.shape
    arrive = pltpu.make_async_copy(own_ref, own, arrived)
    arrive.start()
    steps = written.shape[0]
    chunk = features // steps
    arrive.wait()
    hidden = jnp.concatenate([their_ref[...], own[...]])
    stores = []
    for step in range(steps):
        at = slice(step * chunk, (step + 1) * chunk)
        both = dot(hidden, held_ref[:, at])
        gradient_ref[:, at] = both[:rows] * scale_ref[0:1, 0:1]
        gradient[:, at] = both[rows:]
        stores.append(pltpu.make_async_copy(gradient.at[:, at], own_gradient_ref.at[:, at], written.at[step]))
        stores[step].start()
    for store in stores:
        store.wait()


def partial_kernel(
    place_ref, cotangent_ref, weight_ref, first_ref, second_ref, own_ref, their_ref, held, weight, ready, landed
):
    rows = first_ref.shape[0]
    steps, _, chunk = held.shape
    half = steps // 2
    t, core = place_ref[0], place_ref[1]
    loads, moves = [], []
    for step in range(steps):
        side = core if step < half else 1 - core
        start = (side * half + step % half) * chunk
        spot = pl.ds(pl.multiple_of(start, chunk), chunk)
        loads.append(pltpu.make_async_copy(cotangent_ref.at[:, spot], held.at[step], ready.at[step]))
        spot = pl.ds(pl.multiple_of(t * steps * chunk + start, chunk), chunk)
        moves.append(pltpu.make_async_copy(weight_ref.at[:, spot], weight.at[step], landed.at[step]))
        loads[step].start()
        moves[step].start()
    for step in range(steps):
        source = first_ref if step < half else second_ref
        start = step % half * chunk
        loads[step].wait()
        moves[step].wait()
        product = dot_t(jnp.concatenate([source[:, start : start + chunk], weight[step]]), held[step])
        if step == 0:
            their_ref[...] = product[:rows]
            own_ref[...] = product[rows:]
        else:
            their_ref[...] += product[:rows]
            own_ref[...] += product[rows:]


def add_kernel(left_ref, right_ref, total_ref):
    total_ref[...] = (left_ref[...] + right_ref[...]).astype(total_ref.dtype)


def remainder_kernel(
    place_ref, momentum_ref, own_ref, gradient_ref, inverse_ref, projection_ref,
    remainder_ref, own, carried, left, ready, landed, written,
):
    count, _, chunk = carried.shape
    steps = count // 2
    t = place_ref[0]
    load = pltpu.make_async_copy(own_ref, own, ready)
    moves, stores = [], []
    for step in range(count):
        side = 1 - t if step < steps else t
        spot = pl.ds(pl.multiple_of((side * steps + step % steps) * chunk, chunk), chunk)
        moves.append(pltpu.make_async_copy(momentum_ref.at[:, spot], carried.at[step], landed.at[step]))
        stores.append(pltpu.make_async_copy(left.at[step], remainder_ref.at[:, spot], written.at[step]))
    for copy in moves[:steps] + [load] + moves[steps:]:
        copy.start()
    projection = projection_ref[...].astype(jnp.bfloat16)
    inverse = inverse_ref[0, 0:1, 0:1]
    for step in range(count):
        at = slice(step % steps * chunk, (step % steps + 1) * chunk)
        if step == steps:
            load.wait()
        gradient = gradient_ref[:, at] * inverse if step < steps else own[:, at]
        moves[step].wait()
        accumulated = decay_rate * carried[step] + gradient
        high, low = split(accumulated)
        for block in range(chunk // BLOCK):
            at = slice(block * BLOCK, (block + 1) * BLOCK)
            left[step, :, at] = accumulated[:, at] - band_of(high[:, at], low[:, at], projection)
        stores[step].start()
    for store in stores:
        store.wait()


def thirds(value):
    first = value.astype(jnp.bfloat16).astype(jnp.float32)
    second = (value - first).astype(jnp.bfloat16).astype(jnp.float32)
    return first, second, value - first - second


def finish_kernel(
    summed_ref, cosines_ref, own_ref, far_ref, update_ref, hidden_grad_ref,
    own, far, update, hidden_grad, ready, written,
):
    loads = [
        pltpu.make_async_copy(own_ref, own, ready.at[0]),
        pltpu.make_async_copy(far_ref, far, ready.at[1]),
    ]
    for load in loads:
        load.start()
    cosines = cosines_ref[...].astype(jnp.bfloat16)
    pieces = BAND // summed_ref.shape[1]
    blocks = summed_ref.shape[0] // pieces
    steps = written.shape[0] - 1
    stores = []
    for block in range(blocks):
        parts = [summed_ref[block * pieces + piece] for piece in range(pieces)]
        a, b, c = thirds(jnp.concatenate(parts))
        stacked = jnp.concatenate([a, a, b, b, a, c]).T.astype(jnp.bfloat16)
        update[:, block * BLOCK : (block + 1) * BLOCK] = dot(stacked, cosines).astype(jnp.bfloat16)
        if (block + 1) % (blocks // steps) == 0:
            step = block // (blocks // steps)
            at = pl.ds(step * (blocks // steps) * BLOCK, blocks // steps * BLOCK)
            stores.append(pltpu.make_async_copy(update.at[:, at], update_ref.at[:, at], written.at[step]))
            stores[step].start()
    for load in loads:
        load.wait()
    hidden_grad[...] = (own[...] + far[...]).astype(jnp.bfloat16)
    stores.append(pltpu.make_async_copy(hidden_grad, hidden_grad_ref, written.at[steps]))
    stores[steps].start()
    for store in stores:
        store.wait()


def call(kernel, name, steps, scalars, in_specs, out_specs, out_shape, flops, size, grant=20, **more):
    return pl.pallas_call(
        kernel,
        grid_spec=pltpu.PrefetchScalarGridSpec(
            num_scalar_prefetch=scalars, grid=(steps,), in_specs=in_specs, out_specs=out_specs
        ),
        out_shape=out_shape,
        compiler_params=pltpu.CompilerParams(
            dimension_semantics=("arbitrary",), vmem_limit_bytes=grant << 20
        ),
        cost_estimate=pl.CostEstimate(flops=flops, bytes_accessed=size, transcendentals=0),
        name=name,
        **more,
    )


def whole(shape):
    return pl.BlockSpec(shape, lambda *_: (0,) * len(shape))


def shape_of(*shape, dtype=jnp.float32):
    return jax.ShapeDtypeStruct(shape, dtype)


def vmem_of(*shape):
    return pltpu.VMEM(shape, jnp.float32)


def tables():
    table = cosine_table()
    high, low = halves(table)
    rest = table - high.astype(np.float64) - low.astype(np.float64)
    third = rest.astype(np.float32).astype(jnp.bfloat16)
    cosines = np.concatenate([high, low])
    arrays = (
        cosines,
        np.stack(halves(table.T @ table)),
        np.concatenate([high, low, high, low, third, high]),
    )
    return [array.astype(np.float32) for array in arrays]


def body(hidden, cotangent, down_weight, momentum):
    rows, width = down_weight.shape
    tokens, features = cotangent.shape
    blocks, steps = features // BLOCK, 4
    flops = 2 * rows * tokens * features
    t = lax.axis_index("tensor")
    core = lax.axis_index("core")
    place = jnp.stack([t, core]).astype(jnp.int32)
    cosines, projection, decoder = tables()
    swap = [(0, 1), (1, 0)]
    cross = [(0, 3), (3, 0), (1, 2), (2, 1)]

    momentum = momentum.reshape(rows, width)
    own_hidden = hidden.T
    kept = pltpu.with_memory_space_constraint(own_hidden, pltpu.HBM)
    momentum = pltpu.with_memory_space_constraint(momentum, pltpu.HBM)
    cotangent = pltpu.with_memory_space_constraint(cotangent, pltpu.HBM)
    weights = pltpu.with_memory_space_constraint(down_weight, pltpu.HBM)
    their_hidden = lax.ppermute(own_hidden, "tensor", swap)
    half = features // 2
    sent = lax.dynamic_slice(down_weight, (0, (1 - t) * features + core * half), (rows, half))
    first = lax.ppermute(sent, ("ylo", "tensor"), cross)
    smem = pl.BlockSpec(memory_space=pltpu.SMEM)
    vmem = pl.BlockSpec(memory_space=pltpu.VMEM)
    hbm = pl.BlockSpec(memory_space=pltpu.HBM)
    chunk = features // steps
    own_band, encoded, largest, held = pl.pallas_call(
        own_band_kernel,
        in_specs=[smem, hbm, hbm, hbm, hbm],
        out_specs=[vmem] * 4,
        out_shape=[vmem_of(2 * blocks, BAND, rows), vmem_of(blocks * BAND, tokens), vmem_of(1, features), pltpu.VMEM(cotangent.shape, cotangent.dtype)],
        scratch_shapes=[
            pltpu.VMEM((steps, rows, width // steps), jnp.float32),
            pltpu.VMEM((rows, tokens), hidden.dtype), pltpu.VMEM((2 * BAND, BLOCK), jnp.float32),
            pltpu.SemaphoreType.DMA((steps,)), pltpu.SemaphoreType.DMA((steps,)), pltpu.SemaphoreType.DMA((2,)),
        ],
        compiler_params=pltpu.CompilerParams(vmem_limit_bytes=53 << 20),
        cost_estimate=pl.CostEstimate(flops=flops, bytes_accessed=8 << 20, transcendentals=0),
        name="own_band",
    )(place, kept, cotangent, momentum, cosines)
    near_band = lax.ppermute(own_band, "ylo", swap)

    their_band, scale = call(
        their_band_kernel, "their_band", 1, 0,
        [whole((rows, tokens)), whole((blocks * BAND, tokens)), whole((1, features))],
        [whole((blocks + 1, BAND, rows)), whole((8, 128))],
        [shape_of(blocks + 1, BAND, rows), shape_of(8, 128)],
        4 * rows * tokens * blocks * BAND, 1 << 20, grant=8,
    )(their_hidden, encoded, largest)
    far_band = lax.ppermute(their_band, "tensor", swap)
    cross_band = lax.ppermute(their_band, ("ylo", "tensor"), cross)

    gradient, own_gradient = pl.pallas_call(
        gradients_kernel,
        in_specs=[vmem, hbm, vmem, vmem],
        out_specs=[vmem, hbm],
        out_shape=[vmem_of(rows, features), pltpu.HBM((rows, features), jnp.float32)],
        scratch_shapes=[
            pltpu.VMEM((rows, tokens), hidden.dtype), pltpu.VMEM((rows, features), jnp.float32),
            pltpu.SemaphoreType.DMA, pltpu.SemaphoreType.DMA((4,)),
        ],
        compiler_params=pltpu.CompilerParams(vmem_limit_bytes=16 << 20),
        cost_estimate=pl.CostEstimate(flops=2 * flops, bytes_accessed=6 << 20, transcendentals=0),
        name="gradients",
    )(their_hidden, kept, pltpu.with_memory_space_constraint(held, pltpu.VMEM), scale)
    gradient, near_band, far_band, cross_band = lax.optimization_barrier(
        (gradient, near_band, far_band, cross_band)
    )
    first, gradient = lax.optimization_barrier((first, gradient))
    second = lax.ppermute(first, "core", swap)
    gradient = gradient.astype(jnp.float16)
    far_gradient = lax.ppermute(gradient, "tensor", swap)

    slot = jnp.arange(2)[:, None, None, None]
    received = (far_band + cross_band)[None, :blocks]
    total = (own_band + near_band).reshape(2, blocks, BAND, rows)
    total = total + jnp.where(slot == t, 0.0, received)
    total = total.reshape(64, -1, rows)
    total, gradient = lax.optimization_barrier((total, gradient))
    total_in = total
    total = lax.all_to_all(total, SPACE, 0, 0, tiled=True)

    second, total_in = lax.optimization_barrier((second, total_in))
    own_partial, partial = pl.pallas_call(
        partial_kernel,
        in_specs=[smem, hbm, hbm, vmem, vmem],
        out_specs=[vmem, vmem],
        out_shape=[pltpu.HBM((rows, tokens), jnp.float32), shape_of(rows, tokens)],
        scratch_shapes=[
            pltpu.VMEM((steps, tokens, chunk), cotangent.dtype), pltpu.VMEM((steps, rows, chunk), down_weight.dtype),
            pltpu.SemaphoreType.DMA((steps,)), pltpu.SemaphoreType.DMA((steps,)),
        ],
        compiler_params=pltpu.CompilerParams(vmem_limit_bytes=53 << 20),
        cost_estimate=pl.CostEstimate(flops=1 << 20, bytes_accessed=1 << 12, transcendentals=0),
        name="partials",
    )(place, cotangent, weights, first, second)
    far_gradient, partial = lax.optimization_barrier((far_gradient, partial))
    far_gradient = far_gradient.astype(jnp.float32)
    total, far_gradient, partial = lax.optimization_barrier((total, far_gradient, partial))
    far_partial = lax.ppermute(partial, "tensor", swap)
    total = jnp.sum(total, axis=0)
    summed = lax.all_to_all(jnp.broadcast_to(total[None], (64,) + total.shape), SPACE, 0, 0, tiled=True)

    remainder = pl.pallas_call(
        remainder_kernel,
        in_specs=[smem, hbm, hbm, vmem, vmem, vmem],
        out_specs=hbm,
        out_shape=shape_of(rows, width),
        scratch_shapes=[
            pltpu.VMEM((rows, features), jnp.float32),
            pltpu.VMEM((2 * steps, rows, chunk), jnp.float32), pltpu.VMEM((2 * steps, rows, chunk), jnp.float32),
            pltpu.SemaphoreType.DMA, pltpu.SemaphoreType.DMA((2 * steps,)), pltpu.SemaphoreType.DMA((2 * steps,)),
        ],
        compiler_params=pltpu.CompilerParams(vmem_limit_bytes=53 << 20),
        cost_estimate=pl.CostEstimate(flops=1 << 20, bytes_accessed=1 << 12, transcendentals=0),
        name="remainder",
    )(place, momentum, pltpu.with_memory_space_constraint(own_gradient, pltpu.HBM), far_gradient, far_band[blocks:], projection)

    summed, remainder = lax.optimization_barrier((summed, remainder))
    update, hidden_grad = pl.pallas_call(
        finish_kernel,
        in_specs=[vmem, vmem, hbm, hbm],
        out_specs=[hbm, hbm],
        out_shape=[shape_of(rows, width, dtype=jnp.bfloat16), shape_of(rows, tokens, dtype=jnp.bfloat16)],
        scratch_shapes=[
            pltpu.VMEM((rows, tokens), jnp.float32), pltpu.VMEM((rows, tokens), jnp.float32),
            pltpu.VMEM((rows, width), jnp.bfloat16), pltpu.VMEM((rows, tokens), jnp.bfloat16),
            pltpu.SemaphoreType.DMA((2,)), pltpu.SemaphoreType.DMA((5,)),
        ],
        compiler_params=pltpu.CompilerParams(vmem_limit_bytes=32 << 20),
        name="finish",
    )(summed, decoder, own_partial, far_partial)
    hidden_grad = hidden_grad.T
    return (update, remainder[None], hidden_grad)


def solution(mesh):
    fine = Mesh(mesh.devices.reshape(FINE_SIZES), FINE)
    return jax.shard_map(
        body,
        mesh=fine,
        in_specs=(P(DP, "tensor"), P(DP, "tensor"), P("tensor", None), P(DP, "tensor", None)),
        out_specs=(P("tensor", None), P(DP, "tensor", None), P(DP, "tensor")),
        check_vma=False,
    )
```

```python
import jax
import jax.numpy as jnp
import numpy as np
from jax import lax
from jax.experimental import pallas as pl
from jax.experimental.pallas import tpu as pltpu
from jax.sharding import Mesh
from jax.sharding import PartitionSpec as P

BLOCK = 256
BAND = 8
FINE = ("x", "ylo", "z", "core", "tensor")
FINE_SIZES = (4, 2, 8, 2, 2)
DP = ("x", "ylo", "z", "core")
SPACE = ("x", "z", "core")

decay_rate = 0.9


def cosine_table():
    freq = np.arange(BAND, dtype=np.float64)[:, None]
    place = np.arange(BLOCK, dtype=np.float64)[None, :]
    scales = np.where(freq == 0.0, np.sqrt(1.0 / BLOCK), np.sqrt(2.0 / BLOCK))
    return scales * np.cos(np.pi * (place + 0.5) * freq / BLOCK)


def halves(table):
    high = table.astype(np.float32).astype(jnp.bfloat16)
    low = (table - high.astype(np.float64)).astype(np.float32).astype(jnp.bfloat16)
    return high, low


def split(value):
    high = value.astype(jnp.bfloat16)
    low = (value - high.astype(jnp.float32)).astype(jnp.bfloat16)
    return high, low


def dot(left, right):
    return jnp.dot(left, right, preferred_element_type=jnp.float32)


def dot_t(left, right):
    return lax.dot_general(left, right, (((1,), (1,)), ((), ())), preferred_element_type=jnp.float32)


def encode(high, low, cosines):
    both = dot_t(cosines, high) + dot_t(cosines, low)
    return both[:BAND] + both[BAND:]


def band_of(high, low, projection):
    return dot(high, projection[0]) + dot(low, projection[0]) + dot(high, projection[1])


def own_band_kernel(
    side_ref, hidden_ref, cotangent_ref, momentum_ref, weight_ref, cosines_ref,
    coefficients_ref, encoded_ref, largest_ref, held_ref, partial_ref,
    carried, hidden, table, weight, partial, ready, landed, arrived, written,
):
    steps, features = carried.shape[0], cotangent_ref.shape[1]
    chunk = features // steps
    count, total = chunk // BLOCK, features // BLOCK
    t = side_ref[0]
    loads, moves = [], []
    for step in range(steps):
        at = pl.ds(step * chunk, chunk)
        loads.append(pltpu.make_async_copy(cotangent_ref.at[:, at], held_ref.at[:, at], ready.at[step]))
    for step in range(steps):
        at = pl.ds(step * carried.shape[2], carried.shape[2])
        moves.append(pltpu.make_async_copy(momentum_ref.at[:, at], carried.at[step], landed.at[step]))
    spot = pl.ds(pl.multiple_of(t * features, features), features)
    extra = [
        pltpu.make_async_copy(cosines_ref, table, arrived.at[0]),
        pltpu.make_async_copy(hidden_ref, hidden, arrived.at[1]),
        pltpu.make_async_copy(weight_ref.at[:, spot], weight, arrived.at[2]),
    ]
    for copy in extra[:1] + loads[:1] + extra[2:] + loads[1:] + moves + extra[1:2]:
        copy.start()
    extra[0].wait()
    extra[2].wait()
    cosines = table[...].astype(jnp.bfloat16)
    rows = weight.shape[0]
    zeros = jnp.zeros_like(cosines)
    diagonal = jnp.concatenate([
        jnp.concatenate([cosines if other == block else zeros for other in range(count)], axis=1)
        for block in range(count)
    ])
    for step in range(steps):
        at = slice(step * chunk, (step + 1) * chunk)
        loads[step].wait()
        largest_ref[:, at] = jnp.max(jnp.abs(held_ref[:, at]), axis=0, keepdims=True).astype(jnp.float32)
        product = dot_t(jnp.concatenate([weight[:, at], diagonal]), held_ref[:, at])
        if step == 0:
            partial[...] = product[:rows]
        else:
            partial[...] += product[:rows]
        for block in range(count):
            first = rows + block * 2 * BAND
            place = (step * count + block) * BAND
            encoded_ref[place : place + BAND] = (
                product[first : first + BAND] + product[first + BAND : first + 2 * BAND]
            )
    store = pltpu.make_async_copy(partial, partial_ref, written)
    store.start()
    for step in range(steps):
        moves[step].wait()
        for block in range(carried.shape[2] // BLOCK):
            high, low = split(decay_rate * carried[step, :, block * BLOCK : (block + 1) * BLOCK])
            coefficients_ref[step * (carried.shape[2] // BLOCK) + block] = encode(high, low, cosines)
    extra[1].wait()
    both = dot_t(jnp.concatenate(split(encoded_ref[...])), hidden[...])
    band = both[: total * BAND] + both[total * BAND :]
    for block in range(total):
        coefficients_ref[t * total + block] += band[block * BAND : (block + 1) * BAND]
    store.wait()


def their_band_kernel(hidden_ref, encoded_ref, largest_ref, band_ref, scale_ref):
    hidden = hidden_ref[...]
    count = encoded_ref.shape[0]
    both = dot_t(jnp.concatenate(split(encoded_ref[...])), hidden)
    band = both[:count] + both[count:]
    for block in range(count // BAND):
        band_ref[block] = band[block * BAND : (block + 1) * BAND]
    bound = jnp.max(largest_ref[...]) * jnp.max(jnp.abs(hidden).astype(jnp.float32))
    bound = bound * hidden.shape[1]
    scale, inverse = 1.0, 1.0
    for power in (64, 32, 16, 8, 4, 2):
        fits = bound * (scale * 2.0**power) <= 32768.0
        scale = jnp.where(fits, scale * 2.0**power, scale)
        inverse = jnp.where(fits, inverse * 2.0**-power, inverse)
    scale_ref[...] = jnp.full(scale_ref.shape, scale, jnp.float32)
    band_ref[count // BAND] = jnp.full(band_ref.shape[1:], inverse, jnp.float32)


def gradients_kernel(
    their_ref, own_ref, held_ref, scale_ref, gradient_ref, own_gradient_ref, own, gradient, arrived, written
):
    rows, features = gradient.shape
    arrive = pltpu.make_async_copy(own_ref, own, arrived)
    arrive.start()
    steps = written.shape[0]
    chunk = features // steps
    arrive.wait()
    hidden = jnp.concatenate([their_ref[...], own[...]])
    stores = []
    for step in range(steps):
        at = slice(step * chunk, (step + 1) * chunk)
        both = dot(hidden, held_ref[:, at])
        gradient_ref[:, at] = both[:rows] * scale_ref[0:1, 0:1]
        gradient[:, at] = both[rows:]
        stores.append(pltpu.make_async_copy(gradient.at[:, at], own_gradient_ref.at[:, at], written.at[step]))
        stores[step].start()
    for store in stores:
        store.wait()


def partial_kernel(core_ref, cotangent_ref, first_ref, second_ref, partial_ref, held, ready):
    steps, _, chunk = held.shape
    half = steps // 2
    core = core_ref[0]
    loads = []
    for step in range(steps):
        side = core if step < half else 1 - core
        spot = pl.ds(pl.multiple_of((side * half + step % half) * chunk, chunk), chunk)
        loads.append(pltpu.make_async_copy(cotangent_ref.at[:, spot], held.at[step], ready.at[step]))
        loads[step].start()
    for step in range(steps):
        source = first_ref if step < half else second_ref
        start = step % half * chunk
        loads[step].wait()
        partial = dot_t(source[:, start : start + chunk], held[step])
        if step == 0:
            partial_ref[...] = partial
        else:
            partial_ref[...] += partial


def remainder_kernel(
    side_ref, momentum_ref, own_ref, gradient_ref, inverse_ref, projection_ref,
    remainder_ref, own, carried, left, ready, landed, written,
):
    count, _, chunk = carried.shape
    steps = count // 2
    t = side_ref[0]
    load = pltpu.make_async_copy(own_ref, own, ready)
    moves, stores = [], []
    for step in range(count):
        side = 1 - t if step < steps else t
        spot = pl.ds(pl.multiple_of((side * steps + step % steps) * chunk, chunk), chunk)
        moves.append(pltpu.make_async_copy(momentum_ref.at[:, spot], carried.at[step], landed.at[step]))
        stores.append(pltpu.make_async_copy(left.at[step], remainder_ref.at[:, spot], written.at[step]))
    for copy in moves[:steps] + [load] + moves[steps:]:
        copy.start()
    projection = projection_ref[...].astype(jnp.bfloat16)
    inverse = inverse_ref[0, 0:1, 0:1]
    for step in range(count):
        at = slice(step % steps * chunk, (step % steps + 1) * chunk)
        if step == steps:
            load.wait()
        gradient = gradient_ref[:, at] * inverse if step < steps else own[:, at]
        moves[step].wait()
        accumulated = decay_rate * carried[step] + gradient
        high, low = split(accumulated)
        for block in range(chunk // BLOCK):
            at = slice(block * BLOCK, (block + 1) * BLOCK)
            left[step, :, at] = accumulated[:, at] - band_of(high[:, at], low[:, at], projection)
        stores[step].start()
    for store in stores:
        store.wait()


def add_kernel(left_ref, right_ref, total_ref):
    total_ref[...] = (left_ref[...] + right_ref[...]).astype(total_ref.dtype)


def thirds(value):
    first = value.astype(jnp.bfloat16).astype(jnp.float32)
    second = (value - first).astype(jnp.bfloat16).astype(jnp.float32)
    return first, second, value - first - second


def update_kernel(summed_ref, cosines_ref, update_ref, update, written):
    cosines = cosines_ref[...].astype(jnp.bfloat16)
    steps, _, chunk = update.shape
    count = chunk // BLOCK
    stores = []
    for step in range(steps):
        for block in range(count):
            a, b, c = thirds(summed_ref[step * count + block])
            stacked = jnp.concatenate([a, a, b, b, a, c]).T.astype(jnp.bfloat16)
            at = slice(block * BLOCK, (block + 1) * BLOCK)
            update[step, :, at] = dot(stacked, cosines).astype(jnp.bfloat16)
        at = pl.ds(step * chunk, chunk)
        stores.append(pltpu.make_async_copy(update.at[step], update_ref.at[:, at], written.at[step]))
        stores[step].start()
    for store in stores:
        store.wait()


def call(kernel, name, steps, scalars, in_specs, out_specs, out_shape, flops, size, grant=20, **more):
    return pl.pallas_call(
        kernel,
        grid_spec=pltpu.PrefetchScalarGridSpec(
            num_scalar_prefetch=scalars, grid=(steps,), in_specs=in_specs, out_specs=out_specs
        ),
        out_shape=out_shape,
        compiler_params=pltpu.CompilerParams(
            dimension_semantics=("arbitrary",), vmem_limit_bytes=grant << 20
        ),
        cost_estimate=pl.CostEstimate(flops=flops, bytes_accessed=size, transcendentals=0),
        name=name,
        **more,
    )


def whole(shape):
    return pl.BlockSpec(shape, lambda *_: (0,) * len(shape))


def shape_of(*shape, dtype=jnp.float32):
    return jax.ShapeDtypeStruct(shape, dtype)


def vmem_of(*shape):
    return pltpu.VMEM(shape, jnp.float32)


def tables():
    table = cosine_table()
    high, low = halves(table)
    rest = table - high.astype(np.float64) - low.astype(np.float64)
    third = rest.astype(np.float32).astype(jnp.bfloat16)
    cosines = np.concatenate([high, low])
    arrays = (
        cosines,
        np.stack(halves(table.T @ table)),
        np.concatenate([high, low, high, low, third, high]),
    )
    return [array.astype(np.float32) for array in arrays]


def body(hidden, cotangent, down_weight, momentum):
    rows, width = down_weight.shape
    tokens, features = cotangent.shape
    blocks, steps = features // BLOCK, 4
    flops = 2 * rows * tokens * features
    t = lax.axis_index("tensor")
    core = lax.axis_index("core")
    side, half_at = t.reshape(1), core.reshape(1)
    cosines, projection, decoder = tables()
    swap = [(0, 1), (1, 0)]
    cross = [(0, 3), (3, 0), (1, 2), (2, 1)]

    momentum = momentum.reshape(rows, width)
    own_hidden = hidden.T
    kept = pltpu.with_memory_space_constraint(own_hidden, pltpu.HBM)
    momentum = pltpu.with_memory_space_constraint(momentum, pltpu.HBM)
    cotangent = pltpu.with_memory_space_constraint(cotangent, pltpu.HBM)
    weights = pltpu.with_memory_space_constraint(down_weight, pltpu.HBM)
    their_hidden = lax.ppermute(own_hidden, "tensor", swap)
    half = features // 2
    sent = lax.dynamic_slice(down_weight, (0, (1 - t) * features + core * half), (rows, half))
    first = lax.ppermute(sent, ("ylo", "tensor"), cross)
    smem = pl.BlockSpec(memory_space=pltpu.SMEM)
    vmem = pl.BlockSpec(memory_space=pltpu.VMEM)
    hbm = pl.BlockSpec(memory_space=pltpu.HBM)
    chunk = features // steps
    own_band, encoded, largest, held, own_partial = pl.pallas_call(
        own_band_kernel,
        in_specs=[smem] + [hbm] * 5,
        out_specs=[vmem] * 4 + [hbm],
        out_shape=[
            vmem_of(2 * blocks, BAND, rows), vmem_of(blocks * BAND, tokens), vmem_of(1, features),
            pltpu.VMEM(cotangent.shape, cotangent.dtype), pltpu.HBM((rows, tokens), jnp.float32),
        ],
        scratch_shapes=[
            pltpu.VMEM((steps, rows, width // steps), jnp.float32),
            pltpu.VMEM((rows, tokens), hidden.dtype), pltpu.VMEM((2 * BAND, BLOCK), jnp.float32),
            pltpu.VMEM((rows, features), down_weight.dtype), pltpu.VMEM((rows, tokens), jnp.float32),
            pltpu.SemaphoreType.DMA((steps,)), pltpu.SemaphoreType.DMA((steps,)), pltpu.SemaphoreType.DMA((3,)),
            pltpu.SemaphoreType.DMA,
        ],
        compiler_params=pltpu.CompilerParams(vmem_limit_bytes=53 << 20),
        cost_estimate=pl.CostEstimate(flops=flops, bytes_accessed=8 << 20, transcendentals=0),
        name="own_band",
    )(side, kept, cotangent, momentum, weights, cosines)
    held = pltpu.with_memory_space_constraint(held, pltpu.VMEM)
    near_band = lax.ppermute(own_band, "ylo", swap)

    their_band, scale = call(
        their_band_kernel, "their_band", 1, 0,
        [whole((rows, tokens)), whole((blocks * BAND, tokens)), whole((1, features))],
        [whole((blocks + 1, BAND, rows)), whole((8, 128))],
        [shape_of(blocks + 1, BAND, rows), shape_of(8, 128)],
        4 * rows * tokens * blocks * BAND, 1 << 20, grant=8,
    )(their_hidden, encoded, largest)
    far_band = lax.ppermute(their_band, "tensor", swap)
    cross_band = lax.ppermute(their_band, ("ylo", "tensor"), cross)

    gradient, own_gradient = pl.pallas_call(
        gradients_kernel,
        in_specs=[vmem, hbm, vmem, vmem],
        out_specs=[vmem, hbm],
        out_shape=[vmem_of(rows, features), pltpu.HBM((rows, features), jnp.float32)],
        scratch_shapes=[
            pltpu.VMEM((rows, tokens), hidden.dtype), pltpu.VMEM((rows, features), jnp.float32),
            pltpu.SemaphoreType.DMA, pltpu.SemaphoreType.DMA((4,)),
        ],
        compiler_params=pltpu.CompilerParams(vmem_limit_bytes=16 << 20),
        cost_estimate=pl.CostEstimate(flops=2 * flops, bytes_accessed=6 << 20, transcendentals=0),
        name="gradients",
    )(their_hidden, kept, pltpu.with_memory_space_constraint(held, pltpu.VMEM), scale)
    gradient, near_band, far_band, cross_band = lax.optimization_barrier(
        (gradient, near_band, far_band, cross_band)
    )
    first, gradient = lax.optimization_barrier((first, gradient))
    second = lax.ppermute(first, "core", swap)
    gradient = gradient.astype(jnp.float16)
    far_gradient = lax.ppermute(gradient, "tensor", swap)

    slot = jnp.arange(2)[:, None, None, None]
    received = (far_band + cross_band)[None, :blocks]
    total = (own_band + near_band).reshape(2, blocks, BAND, rows)
    total = total + jnp.where(slot == t, 0.0, received)
    total = total.reshape(64, -1, rows)
    total, gradient = lax.optimization_barrier((total, gradient))
    total_in = total
    total = lax.all_to_all(total, SPACE, 0, 0, tiled=True)

    second, total_in = lax.optimization_barrier((second, total_in))
    partial = pl.pallas_call(
        partial_kernel,
        in_specs=[smem, hbm, vmem, vmem],
        out_specs=vmem,
        out_shape=shape_of(rows, tokens),
        scratch_shapes=[pltpu.VMEM((steps, tokens, chunk), cotangent.dtype), pltpu.SemaphoreType.DMA((steps,))],
        compiler_params=pltpu.CompilerParams(vmem_limit_bytes=53 << 20),
        cost_estimate=pl.CostEstimate(flops=1 << 20, bytes_accessed=1 << 12, transcendentals=0),
        name="their_partial",
    )(half_at, cotangent, first, second)
    far_gradient, partial = lax.optimization_barrier((far_gradient, partial))
    far_gradient = far_gradient.astype(jnp.float32)
    total, far_gradient, partial = lax.optimization_barrier((total, far_gradient, partial))
    far_partial = lax.ppermute(partial, "tensor", swap)
    total = jnp.sum(total, axis=0)
    summed = lax.all_to_all(jnp.broadcast_to(total[None], (64,) + total.shape), SPACE, 0, 0, tiled=True)

    remainder = pl.pallas_call(
        remainder_kernel,
        in_specs=[smem, hbm, hbm, vmem, vmem, vmem],
        out_specs=hbm,
        out_shape=shape_of(rows, width),
        scratch_shapes=[
            pltpu.VMEM((rows, features), jnp.float32),
            pltpu.VMEM((2 * steps, rows, chunk), jnp.float32), pltpu.VMEM((2 * steps, rows, chunk), jnp.float32),
            pltpu.SemaphoreType.DMA, pltpu.SemaphoreType.DMA((2 * steps,)), pltpu.SemaphoreType.DMA((2 * steps,)),
        ],
        compiler_params=pltpu.CompilerParams(vmem_limit_bytes=53 << 20),
        cost_estimate=pl.CostEstimate(flops=1 << 20, bytes_accessed=1 << 12, transcendentals=0),
        name="remainder",
    )(side, momentum, pltpu.with_memory_space_constraint(own_gradient, pltpu.HBM), far_gradient, far_band[blocks:], projection)

    summed, remainder = lax.optimization_barrier((summed, remainder))
    summed = summed.reshape(2 * blocks, BAND, rows)
    update = pl.pallas_call(
        update_kernel,
        in_specs=[vmem, vmem],
        out_specs=hbm,
        out_shape=shape_of(rows, width, dtype=jnp.bfloat16),
        scratch_shapes=[pltpu.VMEM((4, rows, width // 4), jnp.bfloat16), pltpu.SemaphoreType.DMA((4,))],
        compiler_params=pltpu.CompilerParams(vmem_limit_bytes=8 << 20),
        cost_estimate=pl.CostEstimate(flops=1 << 29, bytes_accessed=2 << 20, transcendentals=0),
        name="update",
    )(summed, decoder)

    hidden_grad = call(
        add_kernel, "add", 1, 0, [whole((rows, tokens))] * 2, whole((rows, tokens)),
        shape_of(rows, tokens, dtype=jnp.bfloat16), 1 << 18, 2 << 20,
    )(own_partial, far_partial).T
    return (update, remainder[None], hidden_grad)


def solution(mesh):
    fine = Mesh(mesh.devices.reshape(FINE_SIZES), FINE)
    return jax.shard_map(
        body,
        mesh=fine,
        in_specs=(P(DP, "tensor"), P(DP, "tensor"), P("tensor", None), P(DP, "tensor", None)),
        out_specs=(P("tensor", None), P(DP, "tensor", None), P(DP, "tensor")),
        check_vma=False,
    )
```

```python
import jax
import jax.numpy as jnp
import numpy as np
from jax import lax
from jax.experimental import pallas as pl
from jax.experimental.pallas import tpu as pltpu
from jax.sharding import Mesh
from jax.sharding import PartitionSpec as P

BLOCK = 256
BAND = 8
FINE = ("x", "ylo", "z", "core", "tensor")
FINE_SIZES = (4, 2, 8, 2, 2)
DP = ("x", "ylo", "z", "core")
SPACE = ("x", "z", "core")

decay_rate = 0.9


def cosine_table():
    freq = np.arange(BAND, dtype=np.float64)[:, None]
    place = np.arange(BLOCK, dtype=np.float64)[None, :]
    scales = np.where(freq == 0.0, np.sqrt(1.0 / BLOCK), np.sqrt(2.0 / BLOCK))
    return scales * np.cos(np.pi * (place + 0.5) * freq / BLOCK)


def halves(table):
    high = table.astype(np.float32).astype(jnp.bfloat16)
    low = (table - high.astype(np.float64)).astype(np.float32).astype(jnp.bfloat16)
    return high, low


def split(value):
    high = value.astype(jnp.bfloat16)
    low = (value - high.astype(jnp.float32)).astype(jnp.bfloat16)
    return high, low


def dot(left, right):
    return jnp.dot(left, right, preferred_element_type=jnp.float32)


def dot_t(left, right):
    return lax.dot_general(left, right, (((1,), (1,)), ((), ())), preferred_element_type=jnp.float32)


def encode(high, low, cosines):
    both = dot_t(cosines, high) + dot_t(cosines, low)
    return both[:BAND] + both[BAND:]


def band_of(high, low, projection):
    return dot(high, projection[0]) + dot(low, projection[0]) + dot(high, projection[1])


def own_band_kernel(
    side_ref, hidden_ref, cotangent_ref, momentum_ref, weight_ref, cosines_ref,
    coefficients_ref, encoded_ref, largest_ref, held_ref, partial_ref,
    carried, hidden, table, weight, partial, ready, landed, arrived, written,
):
    steps, features = carried.shape[0], cotangent_ref.shape[1]
    chunk = features // steps
    count, total = chunk // BLOCK, features // BLOCK
    t = side_ref[0]
    loads, moves = [], []
    for step in range(steps):
        at = pl.ds(step * chunk, chunk)
        loads.append(pltpu.make_async_copy(cotangent_ref.at[:, at], held_ref.at[:, at], ready.at[step]))
    for step in range(steps):
        at = pl.ds(step * carried.shape[2], carried.shape[2])
        moves.append(pltpu.make_async_copy(momentum_ref.at[:, at], carried.at[step], landed.at[step]))
    spot = pl.ds(pl.multiple_of(t * features, features), features)
    extra = [
        pltpu.make_async_copy(cosines_ref, table, arrived.at[0]),
        pltpu.make_async_copy(hidden_ref, hidden, arrived.at[1]),
        pltpu.make_async_copy(weight_ref.at[:, spot], weight, arrived.at[2]),
    ]
    for copy in extra[:1] + loads[:1] + extra[2:] + loads[1:] + moves + extra[1:2]:
        copy.start()
    extra[0].wait()
    extra[2].wait()
    cosines = table[...].astype(jnp.bfloat16)
    rows = weight.shape[0]
    zeros = jnp.zeros_like(cosines)
    diagonal = jnp.concatenate([
        jnp.concatenate([cosines if other == block else zeros for other in range(count)], axis=1)
        for block in range(count)
    ])
    for step in range(steps):
        at = slice(step * chunk, (step + 1) * chunk)
        loads[step].wait()
        largest_ref[:, at] = jnp.max(jnp.abs(held_ref[:, at]), axis=0, keepdims=True).astype(jnp.float32)
        product = dot_t(jnp.concatenate([weight[:, at], diagonal]), held_ref[:, at])
        if step == 0:
            partial[...] = product[:rows]
        else:
            partial[...] += product[:rows]
        for block in range(count):
            first = rows + block * 2 * BAND
            place = (step * count + block) * BAND
            encoded_ref[place : place + BAND] = (
                product[first : first + BAND] + product[first + BAND : first + 2 * BAND]
            )
    store = pltpu.make_async_copy(partial, partial_ref, written)
    store.start()
    for step in range(steps):
        moves[step].wait()
        for block in range(carried.shape[2] // BLOCK):
            high, low = split(decay_rate * carried[step, :, block * BLOCK : (block + 1) * BLOCK])
            coefficients_ref[step * (carried.shape[2] // BLOCK) + block] = encode(high, low, cosines)
    extra[1].wait()
    both = dot_t(jnp.concatenate(split(encoded_ref[...])), hidden[...])
    band = both[: total * BAND] + both[total * BAND :]
    for block in range(total):
        coefficients_ref[t * total + block] += band[block * BAND : (block + 1) * BAND]
    store.wait()


def their_band_kernel(hidden_ref, encoded_ref, largest_ref, band_ref, scale_ref):
    hidden = hidden_ref[...]
    count = encoded_ref.shape[0]
    both = dot_t(jnp.concatenate(split(encoded_ref[...])), hidden)
    band = both[:count] + both[count:]
    for block in range(count // BAND):
        band_ref[block] = band[block * BAND : (block + 1) * BAND]
    bound = jnp.max(largest_ref[...]) * jnp.max(jnp.abs(hidden).astype(jnp.float32))
    bound = bound * hidden.shape[1]
    scale, inverse = 1.0, 1.0
    for power in (64, 32, 16, 8, 4, 2):
        fits = bound * (scale * 2.0**power) <= 32768.0
        scale = jnp.where(fits, scale * 2.0**power, scale)
        inverse = jnp.where(fits, inverse * 2.0**-power, inverse)
    scale_ref[...] = jnp.full(scale_ref.shape, scale, jnp.float32)
    band_ref[count // BAND] = jnp.full(band_ref.shape[1:], inverse, jnp.float32)


def gradients_kernel(
    their_ref, own_ref, held_ref, scale_ref, gradient_ref, own_gradient_ref, own, gradient, arrived, written
):
    rows, features = gradient.shape
    arrive = pltpu.make_async_copy(own_ref, own, arrived)
    arrive.start()
    steps = written.shape[0]
    chunk = features // steps
    arrive.wait()
    hidden = jnp.concatenate([their_ref[...], own[...]])
    stores = []
    for step in range(steps):
        at = slice(step * chunk, (step + 1) * chunk)
        both = dot(hidden, held_ref[:, at])
        gradient_ref[:, at] = both[:rows] * scale_ref[0:1, 0:1]
        gradient[:, at] = both[rows:]
        stores.append(pltpu.make_async_copy(gradient.at[:, at], own_gradient_ref.at[:, at], written.at[step]))
        stores[step].start()
    for store in stores:
        store.wait()


def partial_kernel(core_ref, cotangent_ref, first_ref, second_ref, partial_ref, held, ready):
    steps, _, chunk = held.shape
    half = steps // 2
    core = core_ref[0]
    loads = []
    for step in range(steps):
        side = core if step < half else 1 - core
        spot = pl.ds(pl.multiple_of((side * half + step % half) * chunk, chunk), chunk)
        loads.append(pltpu.make_async_copy(cotangent_ref.at[:, spot], held.at[step], ready.at[step]))
        loads[step].start()
    for step in range(steps):
        source = first_ref if step < half else second_ref
        start = step % half * chunk
        loads[step].wait()
        partial = dot_t(source[:, start : start + chunk], held[step])
        if step == 0:
            partial_ref[...] = partial
        else:
            partial_ref[...] += partial


def remainder_kernel(
    side_ref, momentum_ref, own_ref, gradient_ref, inverse_ref, projection_ref,
    remainder_ref, own, carried, left, ready, landed, written,
):
    count, _, chunk = carried.shape
    steps = count // 2
    t = side_ref[0]
    load = pltpu.make_async_copy(own_ref, own, ready)
    moves, stores = [], []
    for step in range(count):
        side = 1 - t if step < steps else t
        spot = pl.ds(pl.multiple_of((side * steps + step % steps) * chunk, chunk), chunk)
        moves.append(pltpu.make_async_copy(momentum_ref.at[:, spot], carried.at[step], landed.at[step]))
        stores.append(pltpu.make_async_copy(left.at[step], remainder_ref.at[:, spot], written.at[step]))
    for copy in moves[:steps] + [load] + moves[steps:]:
        copy.start()
    projection = projection_ref[...].astype(jnp.bfloat16)
    inverse = inverse_ref[0, 0:1, 0:1]
    for step in range(count):
        at = slice(step % steps * chunk, (step % steps + 1) * chunk)
        if step == steps:
            load.wait()
        gradient = gradient_ref[:, at] * inverse if step < steps else own[:, at]
        moves[step].wait()
        accumulated = decay_rate * carried[step] + gradient
        high, low = split(accumulated)
        for block in range(chunk // BLOCK):
            at = slice(block * BLOCK, (block + 1) * BLOCK)
            left[step, :, at] = accumulated[:, at] - band_of(high[:, at], low[:, at], projection)
        stores[step].start()
    for store in stores:
        store.wait()


def add_kernel(left_ref, right_ref, total_ref):
    total_ref[...] = (left_ref[...] + right_ref[...]).astype(total_ref.dtype)


def thirds(value):
    first = value.astype(jnp.bfloat16).astype(jnp.float32)
    second = (value - first).astype(jnp.bfloat16).astype(jnp.float32)
    return first, second, value - first - second


def update_kernel(summed_ref, cosines_ref, update_ref, update, written):
    cosines = cosines_ref[...].astype(jnp.bfloat16)
    steps, _, chunk = update.shape
    count = chunk // BLOCK
    stores = []
    for step in range(steps):
        for block in range(count):
            a, b, c = thirds(summed_ref[step * count + block])
            stacked = jnp.concatenate([a, a, b, b, a, c]).T.astype(jnp.bfloat16)
            at = slice(block * BLOCK, (block + 1) * BLOCK)
            update[step, :, at] = dot(stacked, cosines).astype(jnp.bfloat16)
        at = pl.ds(step * chunk, chunk)
        stores.append(pltpu.make_async_copy(update.at[step], update_ref.at[:, at], written.at[step]))
        stores[step].start()
    for store in stores:
        store.wait()


def call(kernel, name, steps, scalars, in_specs, out_specs, out_shape, flops, size, grant=20, **more):
    return pl.pallas_call(
        kernel,
        grid_spec=pltpu.PrefetchScalarGridSpec(
            num_scalar_prefetch=scalars, grid=(steps,), in_specs=in_specs, out_specs=out_specs
        ),
        out_shape=out_shape,
        compiler_params=pltpu.CompilerParams(
            dimension_semantics=("arbitrary",), vmem_limit_bytes=grant << 20
        ),
        cost_estimate=pl.CostEstimate(flops=flops, bytes_accessed=size, transcendentals=0),
        name=name,
        **more,
    )


def whole(shape):
    return pl.BlockSpec(shape, lambda *_: (0,) * len(shape))


def shape_of(*shape, dtype=jnp.float32):
    return jax.ShapeDtypeStruct(shape, dtype)


def vmem_of(*shape):
    return pltpu.VMEM(shape, jnp.float32)


def tables():
    table = cosine_table()
    high, low = halves(table)
    rest = table - high.astype(np.float64) - low.astype(np.float64)
    third = rest.astype(np.float32).astype(jnp.bfloat16)
    cosines = np.concatenate([high, low])
    arrays = (
        cosines,
        np.stack(halves(table.T @ table)),
        np.concatenate([high, low, high, low, third, high]),
    )
    return [array.astype(np.float32) for array in arrays]


def body(hidden, cotangent, down_weight, momentum):
    rows, width = down_weight.shape
    tokens, features = cotangent.shape
    blocks, steps = features // BLOCK, 4
    flops = 2 * rows * tokens * features
    t = lax.axis_index("tensor")
    core = lax.axis_index("core")
    side, half_at = t.reshape(1), core.reshape(1)
    cosines, projection, decoder = tables()
    swap = [(0, 1), (1, 0)]
    cross = [(0, 3), (3, 0), (1, 2), (2, 1)]

    momentum = momentum.reshape(rows, width)
    own_hidden = hidden.T
    kept = pltpu.with_memory_space_constraint(own_hidden, pltpu.HBM)
    momentum = pltpu.with_memory_space_constraint(momentum, pltpu.HBM)
    cotangent = pltpu.with_memory_space_constraint(cotangent, pltpu.HBM)
    weights = pltpu.with_memory_space_constraint(down_weight, pltpu.HBM)
    their_hidden = lax.ppermute(own_hidden, "tensor", swap)
    half = features // 2
    sent = lax.dynamic_slice(down_weight, (0, (1 - t) * features + core * half), (rows, half))
    first = lax.ppermute(sent, ("ylo", "tensor"), cross)
    smem = pl.BlockSpec(memory_space=pltpu.SMEM)
    vmem = pl.BlockSpec(memory_space=pltpu.VMEM)
    hbm = pl.BlockSpec(memory_space=pltpu.HBM)
    chunk = features // steps
    own_band, encoded, largest, held, own_partial = pl.pallas_call(
        own_band_kernel,
        in_specs=[smem] + [hbm] * 5,
        out_specs=[vmem] * 4 + [hbm],
        out_shape=[
            vmem_of(2 * blocks, BAND, rows), vmem_of(blocks * BAND, tokens), vmem_of(1, features),
            pltpu.VMEM(cotangent.shape, cotangent.dtype), pltpu.HBM((rows, tokens), jnp.float32),
        ],
        scratch_shapes=[
            pltpu.VMEM((steps, rows, width // steps), jnp.float32),
            pltpu.VMEM((rows, tokens), hidden.dtype), pltpu.VMEM((2 * BAND, BLOCK), jnp.float32),
            pltpu.VMEM((rows, features), down_weight.dtype), pltpu.VMEM((rows, tokens), jnp.float32),
            pltpu.SemaphoreType.DMA((steps,)), pltpu.SemaphoreType.DMA((steps,)), pltpu.SemaphoreType.DMA((3,)),
            pltpu.SemaphoreType.DMA,
        ],
        compiler_params=pltpu.CompilerParams(vmem_limit_bytes=53 << 20),
        cost_estimate=pl.CostEstimate(flops=flops, bytes_accessed=8 << 20, transcendentals=0),
        name="own_band",
    )(side, kept, cotangent, momentum, weights, cosines)
    held = pltpu.with_memory_space_constraint(held, pltpu.VMEM)
    near_band = lax.ppermute(own_band, "ylo", swap)

    their_band, scale = call(
        their_band_kernel, "their_band", 1, 0,
        [whole((rows, tokens)), whole((blocks * BAND, tokens)), whole((1, features))],
        [whole((blocks + 1, BAND, rows)), whole((8, 128))],
        [shape_of(blocks + 1, BAND, rows), shape_of(8, 128)],
        4 * rows * tokens * blocks * BAND, 1 << 20, grant=8,
    )(their_hidden, encoded, largest)
    far_band = lax.ppermute(their_band, "tensor", swap)
    cross_band = lax.ppermute(their_band, ("ylo", "tensor"), cross)

    gradient, own_gradient = pl.pallas_call(
        gradients_kernel,
        in_specs=[vmem, hbm, vmem, vmem],
        out_specs=[vmem, hbm],
        out_shape=[vmem_of(rows, features), pltpu.HBM((rows, features), jnp.float32)],
        scratch_shapes=[
            pltpu.VMEM((rows, tokens), hidden.dtype), pltpu.VMEM((rows, features), jnp.float32),
            pltpu.SemaphoreType.DMA, pltpu.SemaphoreType.DMA((4,)),
        ],
        compiler_params=pltpu.CompilerParams(vmem_limit_bytes=16 << 20),
        cost_estimate=pl.CostEstimate(flops=2 * flops, bytes_accessed=6 << 20, transcendentals=0),
        name="gradients",
    )(their_hidden, kept, pltpu.with_memory_space_constraint(held, pltpu.VMEM), scale)
    gradient, near_band, far_band, cross_band = lax.optimization_barrier(
        (gradient, near_band, far_band, cross_band)
    )
    first, gradient = lax.optimization_barrier((first, gradient))
    second = lax.ppermute(first, "core", swap)
    gradient = gradient.astype(jnp.float16)
    far_gradient = lax.ppermute(gradient, "tensor", swap)

    slot = jnp.arange(2)[:, None, None, None]
    received = (far_band + cross_band)[None, :blocks]
    total = (own_band + near_band).reshape(2, blocks, BAND, rows)
    total = total + jnp.where(slot == t, 0.0, received)
    total = total.reshape(64, -1, rows)
    total, gradient = lax.optimization_barrier((total, gradient))
    total_in = total
    total = lax.all_to_all(total, SPACE, 0, 0, tiled=True)

    second, total_in = lax.optimization_barrier((second, total_in))
    partial = pl.pallas_call(
        partial_kernel,
        in_specs=[smem, hbm, vmem, vmem],
        out_specs=vmem,
        out_shape=shape_of(rows, tokens),
        scratch_shapes=[pltpu.VMEM((steps, tokens, chunk), cotangent.dtype), pltpu.SemaphoreType.DMA((steps,))],
        compiler_params=pltpu.CompilerParams(vmem_limit_bytes=53 << 20),
        cost_estimate=pl.CostEstimate(flops=1 << 20, bytes_accessed=1 << 12, transcendentals=0),
        name="their_partial",
    )(half_at, cotangent, first, second)
    far_gradient, partial = lax.optimization_barrier((far_gradient, partial))
    far_gradient = far_gradient.astype(jnp.float32)
    far_partial = lax.ppermute(partial, "tensor", swap)
    total = jnp.sum(total, axis=0)
    summed = lax.all_to_all(jnp.broadcast_to(total[None], (64,) + total.shape), SPACE, 0, 0, tiled=True)

    remainder = pl.pallas_call(
        remainder_kernel,
        in_specs=[smem, hbm, hbm, vmem, vmem, vmem],
        out_specs=hbm,
        out_shape=shape_of(rows, width),
        scratch_shapes=[
            pltpu.VMEM((rows, features), jnp.float32),
            pltpu.VMEM((2 * steps, rows, chunk), jnp.float32), pltpu.VMEM((2 * steps, rows, chunk), jnp.float32),
            pltpu.SemaphoreType.DMA, pltpu.SemaphoreType.DMA((2 * steps,)), pltpu.SemaphoreType.DMA((2 * steps,)),
        ],
        compiler_params=pltpu.CompilerParams(vmem_limit_bytes=53 << 20),
        cost_estimate=pl.CostEstimate(flops=6442450944, bytes_accessed=1 << 12, transcendentals=0),
        name="remainder",
    )(side, momentum, pltpu.with_memory_space_constraint(own_gradient, pltpu.HBM), far_gradient, far_band[blocks:], projection)

    summed, remainder = lax.optimization_barrier((summed, remainder))
    summed = summed.reshape(2 * blocks, BAND, rows)
    update = pl.pallas_call(
        update_kernel,
        in_specs=[vmem, vmem],
        out_specs=hbm,
        out_shape=shape_of(rows, width, dtype=jnp.bfloat16),
        scratch_shapes=[pltpu.VMEM((4, rows, width // 4), jnp.bfloat16), pltpu.SemaphoreType.DMA((4,))],
        compiler_params=pltpu.CompilerParams(vmem_limit_bytes=8 << 20),
        cost_estimate=pl.CostEstimate(flops=1 << 29, bytes_accessed=2 << 20, transcendentals=0),
        name="update",
    )(summed, decoder)

    hidden_grad = call(
        add_kernel, "add", 1, 0, [whole((rows, tokens))] * 2, whole((rows, tokens)),
        shape_of(rows, tokens, dtype=jnp.bfloat16), 1 << 18, 2 << 20,
    )(own_partial, far_partial).T
    return (update, remainder[None], hidden_grad)


def solution(mesh):
    fine = Mesh(mesh.devices.reshape(FINE_SIZES), FINE)
    return jax.shard_map(
        body,
        mesh=fine,
        in_specs=(P(DP, "tensor"), P(DP, "tensor"), P("tensor", None), P(DP, "tensor", None)),
        out_specs=(P("tensor", None), P(DP, "tensor", None), P(DP, "tensor")),
        check_vma=False,
    )
```
